32 devices in a mesh: dom: 32 (over z, y, x, core).
Axes of the slice: x: 2, y: 2, z: 4, core: 2. Of those that a mesh axis runs over, the one named last changes fastest.
Arguments:
- positions: float32 [32, 3, 2048], P('dom'), may hold values from -6 to 6
- states: float32 [32, 5, 27, 256], P('dom'), may hold values from -6 to 6
- conn: int32 [32, 27, 256], P('dom'), may hold values from 0 to 2047
- send_nodes: int32 [32, 4, 32], P('dom'), may hold values from 0 to 2047
- recv_nodes: int32 [32, 4, 32], P('dom'), may hold values from 0 to 2047
- send_elems: int32 [32, 4, 16], P('dom'), may hold values from 0 to 255
- neighbours: int32 [32, 6, 256], P('dom'), may hold values from 0 to 319
- live: int32 [32], P('dom'), may hold values from 128 to 256, as said below
- smooth: float32 [27, 27], replicated, may hold values from -1.25 to 1.25
- face_geo: float32 [6, 3, 27], replicated, may hold values from -0.625 to 0.625
- rates: float32 [32, 6, 256], P('dom'), may hold values from 0.1 to 1
- stiff: float32 [27, 27], replicated, may hold values from -1.25 to 1.25
- lift: float32 [6, 27, 27], replicated, may hold values from -1.25 to 1.25
- mass_inv: float32 [27, 27], replicated, may hold values from -1.25 to 1.25
Outputs:
- coords: float32 [32, 3, 2048], P('dom')
- remapped: float32 [32, 5, 27, 256], P('dom')
The draws below stay inside these ranges and needn't reach their ends.
Inputs may be any that keep to these rules, and one draw needn't show every extreme that they name: Elements from live[p] on are padding; at least one partition is full.
All inputs are finite; a program needn't handle non-finite values.
Results may differ from the reference program's by a relative error of at most 0.0001.
Values sent between devices are 32-bit elements; how exact they have to be, the bound alone decides.
A program may use at most 64 MiB of HBM per device.

```python
import math
import jax
import jax.numpy as jnp
from jax import lax

E_DEV = 256
BASIS = 27
FIELDS = 5
FACES = 6
SWEEPS = 3
STEPS = 4
NODES_DEV = 2048
GHOSTS = 16
SHARED = 32
PARTS_SIZE = 32


def draw_live(key, part):
    base = jax.random.randint(key, (PARTS_SIZE,), E_DEV // 2, E_DEV + 1)
    chosen = jax.random.randint(jax.random.fold_in(key, 7), (), 0, PARTS_SIZE)
    return jnp.where(jnp.arange(PARTS_SIZE) == chosen, E_DEV, base).astype(jnp.int32)


def with_ends(array, key, smallest, top_value):
    dims = array.shape
    spot = [jax.random.randint(jax.random.fold_in(key, axis), (), 0, dims[axis]) for axis in range(len(dims))]
    array = array.at[tuple(spot)].set(smallest)
    longest = dims.index(max(dims))
    spot[longest] = (spot[longest] + 1) % dims[longest]
    return array.at[tuple(spot)].set(top_value)


def level_of(key, dims, shards, low, high):
    def one(dim, blocks):
        steps = jax.random.uniform(jax.random.fold_in(jax.random.fold_in(key, 6), dim), (blocks,), jnp.float32, low / len(shards), high / len(shards))
        return jnp.repeat(jnp.exp(steps), dims[dim] // blocks).reshape((-1,) + (1,) * (len(dims) - dim - 1))

    level = one(*shards[0])
    for cut in shards[1:]:
        level = level * one(*cut)
    return level


def noise(stream_key, dims, scale, most, pieces=(), held_as=jnp.bfloat16):
    factor_of = level_of(stream_key, dims, pieces, -0.22, 0.18) if pieces else 1.0
    result = jax.random.normal(stream_key, dims, jnp.float32) * scale * factor_of
    return jnp.minimum(jnp.maximum(result, -most), most).astype(held_as)


def setup_inputs(seed: int = 0) -> dict:
    arg_keys = jax.random.split(jax.random.key(seed), 15)
    return {
        "positions": noise(arg_keys[0], (PARTS_SIZE, 3, NODES_DEV), 1.0, 6.0, ((0, 32),), jnp.float32),
        "states": noise(arg_keys[1], (PARTS_SIZE, FIELDS, BASIS, E_DEV), 1.0, 6.0, ((0, 32),), jnp.float32),
        "conn": with_ends(jax.random.randint(arg_keys[2], (PARTS_SIZE, BASIS, E_DEV), 0, NODES_DEV), jax.random.fold_in(arg_keys[2], 1), 0, NODES_DEV - 1).astype(jnp.int32),
        "send_nodes": with_ends(jax.random.randint(arg_keys[3], (PARTS_SIZE, 4, SHARED), 0, NODES_DEV), jax.random.fold_in(arg_keys[3], 1), 0, NODES_DEV - 1).astype(jnp.int32),
        "recv_nodes": with_ends(jax.random.randint(arg_keys[4], (PARTS_SIZE, 4, SHARED), 0, NODES_DEV), jax.random.fold_in(arg_keys[4], 1), 0, NODES_DEV - 1).astype(jnp.int32),
        "send_elems": with_ends(jax.random.randint(arg_keys[5], (PARTS_SIZE, 4, GHOSTS), 0, E_DEV), jax.random.fold_in(arg_keys[5], 1), 0, E_DEV - 1).astype(jnp.int32),
        "neighbours": with_ends(jax.random.randint(arg_keys[6], (PARTS_SIZE, FACES, E_DEV), 0, E_DEV + 4 * GHOSTS), jax.random.fold_in(arg_keys[6], 1), 0, (E_DEV + 4 * GHOSTS) - 1).astype(jnp.int32),
        "live": draw_live(jax.random.fold_in(arg_keys[14], 71), 0),
        "smooth": noise(arg_keys[8], (BASIS, BASIS), BASIS ** -0.5, 1.25, (), jnp.float32),
        "face_geo": noise(arg_keys[9], (FACES, 3, BASIS), (3 * BASIS) ** -0.5, 0.625, (), jnp.float32),
        "rates": jnp.clip(jnp.exp(math.log(1.0) - 2.3025851 * jax.random.uniform(arg_keys[10], (PARTS_SIZE, FACES, E_DEV), jnp.float32) ** level_of(arg_keys[10], (PARTS_SIZE, FACES, E_DEV), ((0, 32),), -0.2, 0.2)), 0.1, 1.0),
        "stiff": noise(arg_keys[11], (BASIS, BASIS), BASIS ** -0.5, 1.25, (), jnp.float32),
        "lift": noise(arg_keys[12], (FACES, BASIS, BASIS), BASIS ** -0.5, 1.25, (), jnp.float32),
        "mass_inv": noise(arg_keys[13], (BASIS, BASIS), BASIS ** -0.5, 1.25, (), jnp.float32),
    }


relax_factor = 0.5
cfl_number = 0.4
highest = lax.Precision.HIGHEST


def neighbour_offsets(parts):
    stride = max(parts // 8, 1)
    return (1, -1, stride, -stride)


def node_counts(connect, receive, mask, nodes):
    weights = jnp.broadcast_to(mask[None, :], connect.shape).reshape(-1)
    counted = jnp.zeros((nodes,), jnp.float32).at[connect.reshape(-1)].add(weights)
    counted = counted.at[receive.reshape(-1)].add(jnp.ones((receive.size,), jnp.float32))
    return jnp.maximum(counted, 1.0)


def assemble(coords, connect, mask, smooth):
    corner = coords[:, connect]
    smoothed = jnp.einsum('ab,cbe->cae', smooth, corner, precision=highest) * mask[None, None, :]
    flat = smoothed.reshape(coords.shape[0], -1)
    return jnp.zeros(coords.shape, jnp.float32).at[:, connect.reshape(-1)].add(flat)


def face_rates(moved, connect, face_geo, rates, mask):
    corner = moved[:, connect]
    projected = jnp.einsum('fca,cae->fe', face_geo, corner, precision=highest)
    return rates * (1.0 + 0.5 * jnp.tanh(projected)) * mask[None, :]


def advance(values, extended, neighbour, rate, mask, step_size, stiff, lift, mass_inv):
    flux = jnp.einsum('ab,vbe->vae', stiff, values, precision=highest)
    for face in range(6):
        other = jnp.take(extended, neighbour[face], axis=2)
        flux = flux + rate[face][None, None, :] * jnp.einsum('ab,vbe->vae', lift[face], other - values, precision=highest)
    change = jnp.einsum('ab,vbe->vae', mass_inv, flux, precision=highest)
    return values + step_size * change * mask[None, None, :]


def reference(positions, states, conn, send_nodes, recv_nodes, send_elems, neighbours, live, smooth, face_geo, rates, stiff, lift, mass_inv):
    parts = positions.shape[0]
    shifts = neighbour_offsets(parts)
    elems = conn.shape[-1]
    nodes = positions.shape[-1]
    mask = (jnp.arange(elems)[None, :] < live[:, None]).astype(jnp.float32)
    counts = lax.map(lambda item: node_counts(item[0], item[1], item[2], nodes), (conn, recv_nodes, mask))
    coords = positions
    for sweep in range(SWEEPS):
        summed = lax.map(lambda item: assemble(item[0], item[1], item[2], smooth), (coords, conn, mask))
        total = summed
        for k in range(4):
            picked = jax.vmap(lambda rows, index: rows[:, index])(summed, send_nodes[:, k])
            arrived = jnp.roll(picked, shifts[k], axis=0)
            total = jax.vmap(lambda acc, index, add: acc.at[:, index].add(add))(total, recv_nodes[:, k], arrived)
        coords = coords + relax_factor * (total / counts[:, None, :] - coords)
    moved = coords - positions
    rate = lax.map(lambda item: face_rates(item[0], item[1], face_geo, item[2], item[3]), (moved, conn, rates, mask))
    step_size = cfl_number / jnp.max(jnp.sum(rate, axis=1))
    values = states
    for step in range(STEPS):
        ghosts = []
        for k in range(4):
            picked = jax.vmap(lambda vals, index: vals[:, :, index])(values, send_elems[:, k])
            ghosts.append(jnp.roll(picked, shifts[k], axis=0))
        extended = jnp.concatenate([values] + ghosts, axis=3)
        values = lax.map(lambda item: advance(item[0], item[1], item[2], item[3], item[4], step_size, stiff, lift, mass_inv), (values, extended, neighbours, rate, mask))
    return coords, values
```

```python
import functools

import jax
import jax.numpy as jnp
from jax import lax
from jax.experimental import pallas as pl
from jax.experimental.pallas import tpu as pltpu
from jax.sharding import PartitionSpec as P

SWEEPS = 3
STEPS = 4
CFL = 0.4
F32 = jnp.float32
BF16 = jnp.bfloat16
HIGHEST = lax.Precision.HIGHEST
MESH = pl.DeviceIdType.MESH
LANES = 128
ROWS = 32
RADIX = 32


def rounds_of(parts):
    found, stride = [], 1
    while parts > 1:
        radix = max(r for r in range(1, RADIX + 1) if parts % r == 0)
        if radix == 1:
            radix = parts
        found.append((radix, stride))
        stride *= radix
        parts //= radix
    return found


def pick(table, index):
    return jnp.take_along_axis(table, index, axis=1, mode="promise_in_bounds")


def split(x):
    high = x.astype(BF16)
    low = (x - high.astype(F32)).astype(BF16)
    return high, low


def mm(a, b):
    return jnp.dot(a, b, preferred_element_type=F32)


def mm3(a, b):
    high, low = split(b)
    return mm(a[0], high) + (mm(a[1], high) + mm(a[0], low))


def mm_nt(a, b):
    return lax.dot_general(a, b, (((1,), (1,)), ((), ())), preferred_element_type=F32)


def iota(shape, dim):
    return lax.broadcasted_iota(jnp.int32, shape, dim)


def kernel(
    parts, shifts, rounds,
    pos, states, conn, send_nodes, recv_nodes, send_elems, neighbours, live,
    smooth, face_geo, rates, stiff, lift, mass_inv,
    out_c, out_u,
    x_ref, x0_ref, s_ref, lo_ref, hi_ref, y_ref, z_ref, b_ref, rb_ref,
    u_ref, nb_ref, rate_ref, pad_ref, fg_ref, w_ref, idx_ref,
    v_send, v_recv, g_send, g_recv, m_send, m_recv,
    vs_sem, vr_sem, gs_sem, gr_sem, ms_sem, mr_sem,
):
    me = lax.axis_index("dom")
    basis, elems = conn.shape[1], conn.shape[2]
    fields = states.shape[1]
    faces = neighbours.shape[1]
    nodes = pos.shape[2]
    groups = nodes // LANES
    halves = elems // LANES
    shared = send_nodes.shape[2]
    ghosts = send_elems.shape[2]
    slots = LANES // ghosts

    partners = []
    for radix, stride in rounds:
        digit = lax.rem(me // stride, radix)
        partners.append(
            [me + (lax.rem(digit + j, radix) - digit) * stride for j in range(1, radix)]
        )
    targets = [lax.rem(me + o + parts, parts) for o in shifts]

    barrier = pltpu.get_barrier_semaphore()
    greeted = targets + [t for one in partners for t in one]
    for t in greeted:
        pl.semaphore_signal(barrier, inc=1, device_id=(t,), device_id_type=MESH)

    u_ref[...] = jnp.zeros(u_ref.shape, F32)
    for v in range(fields):
        u_ref[v * ROWS : v * ROWS + basis, :] = states[0, v]

    lane = iota((8, LANES), 1)
    row = iota((8, LANES), 0)
    idx_ref[...] = jnp.zeros(idx_ref.shape, jnp.int32)
    idx_ref[0:4, 0:shared] = send_nodes[0]
    idx_ref[8:12, 0:shared] = recv_nodes[0]
    idx_ref[16:20, 0:ghosts] = send_elems[0]

    def flat(block):
        spread = pick(block, lax.rem(lane, shared))
        kept = jnp.where(lane // shared == row, spread, 0)
        return jnp.sum(kept, axis=0, keepdims=True)

    sent_nodes = flat(idx_ref[0:8, :])
    got_nodes = flat(idx_ref[8:16, :])
    idx_ref[16:24, :] = pick(idx_ref[16:24, :], lax.rem(lane, ghosts))

    slot_of = iota((ROWS, LANES), 1) // ghosts

    def pack_ghosts(step):
        for k in range(4):
            which = jnp.broadcast_to(idx_ref[16 + k : 17 + k, :], (ROWS, LANES))
            low = which & (LANES - 1)
            far = which >> 7
            tile = jnp.zeros((ROWS, LANES), F32)
            for v in range(fields):
                got = pick(u_ref[v * ROWS : (v + 1) * ROWS, 0:LANES], low)
                for h in range(1, halves):
                    other = pick(u_ref[v * ROWS : (v + 1) * ROWS, h * LANES : (h + 1) * LANES], low)
                    got = jnp.where(far == h, other, got)
                tile = jnp.where(slot_of == (v + k) % slots, got, tile)
            g_send[step, k] = tile

    def ghost_copy(step, k):
        return pltpu.make_async_remote_copy(
            src_ref=g_send.at[step, k], dst_ref=g_recv.at[step, k],
            send_sem=gs_sem.at[step, k], recv_sem=gr_sem.at[step, k],
            device_id=(targets[k],), device_id_type=MESH,
        )

    def node_copy(sweep, k):
        return pltpu.make_async_remote_copy(
            src_ref=v_send.at[sweep], dst_ref=v_recv.at[sweep, k],
            send_sem=vs_sem.at[sweep, k], recv_sem=vr_sem.at[sweep, k],
            device_id=(targets[k],), device_id_type=MESH,
        )

    def most_copy(r, j):
        at = sum(len(p) for p in partners[:r]) + j
        return pltpu.make_async_remote_copy(
            src_ref=m_send.at[r], dst_ref=m_recv.at[at],
            send_sem=ms_sem.at[at], recv_sem=mr_sem.at[at],
            device_id=(partners[r][j],), device_id_type=MESH,
        )

    pack_ghosts(0)

    for c in range(3):
        for g in range(groups):
            r = c * groups + g
            x0_ref[r : r + 1, :] = pos[0, c : c + 1, g * LANES : (g + 1) * LANES]
    x_ref[...] = x0_ref[...]
    s_ref[...] = jnp.zeros(s_ref.shape, F32)

    alive = (iota((1, elems), 1) < live[0])
    lo_ref[...] = jnp.zeros(lo_ref.shape, jnp.int32)
    hi_ref[...] = jnp.zeros(hi_ref.shape, jnp.int32)
    lo_ref[0:basis, :] = conn[0] & (LANES - 1)
    hi_ref[0:basis, :] = conn[0] >> 7

    sub_lo = iota((LANES, elems), 0)
    sub_hi = iota((groups, elems), 0)
    one_lo, one_hi = jnp.float32(1.0), jnp.float32(1.0)
    for a in range(basis):
        at = pl.ds(a * elems, elems)
        b_ref[:, at] = jnp.where(sub_lo == lo_ref[a : a + 1, :], one_lo, 0.0).astype(BF16)
        z_ref[0:groups, at] = jnp.where(
            jnp.where(alive, hi_ref[a : a + 1, :], groups) == sub_hi, one_hi, 0.0
        ).astype(BF16)
    got_lo, got_hi = got_nodes & (LANES - 1), got_nodes >> 7
    rb_ref[...] = jnp.where(iota((LANES, LANES), 0) == got_lo, one_lo, 0.0).astype(BF16)
    got_mask = iota((groups, LANES), 0) == got_hi
    count = mm_nt(z_ref[0:groups, :], b_ref[...])
    count = count + mm_nt(jnp.where(got_mask, one_hi, 0.0).astype(BF16), rb_ref[...])
    half_inv = 0.5 / jnp.maximum(count, 1.0)
    half_inv = jnp.concatenate([half_inv] * 3, axis=0)

    pl.semaphore_wait(barrier, len(greeted))
    for k in range(4):
        ghost_copy(0, k).start()

    pad_ref[...] = jnp.zeros(pad_ref.shape, F32)
    for i in range(faces + 1):
        matrix = stiff[...] if i == 0 else lift[i - 1]
        pad_ref[i * ROWS : i * ROWS + basis, 0:basis] = jnp.dot(
            mass_inv[...], matrix, precision=HIGHEST, preferred_element_type=F32
        )
    wide = []
    for first in range(0, faces + 1, 4):
        total = None
        for i in range(first, min(first + 4, faces + 1)):
            block = pad_ref[i * ROWS : (i + 1) * ROWS, :]
            if i > first:
                block = pltpu.roll(block, ROWS * (i - first), 1)
            total = block if total is None else total + block
        wide.append(total)
    w_high, w_low = split(jnp.concatenate(wide, axis=1))
    w_ref[0:ROWS, :] = w_high
    w_ref[ROWS : 2 * ROWS, :] = w_low
    pad_ref[0:ROWS, :] = jnp.zeros((ROWS, LANES), F32)
    pad_ref[0:basis, 0:basis] = smooth[...]
    smooth_parts = split(pad_ref[0:ROWS, 0:ROWS])
    fg_ref[...] = jnp.zeros(fg_ref.shape, F32)
    for c in range(3):
        fg_ref[c * 8 : c * 8 + faces, 0:basis] = face_geo[:, c, :]

    def corners(table):
        result = []
        for c in range(3):
            cols = []
            for h in range(halves):
                low = lo_ref[:, h * LANES : (h + 1) * LANES]
                high = hi_ref[:, h * LANES : (h + 1) * LANES]
                value = jnp.zeros((ROWS, LANES), F32)
                for g in range(groups):
                    r = c * groups + g
                    source = jnp.broadcast_to(table[r : r + 1, :], (ROWS, LANES))
                    value = jnp.where(high == g, pick(source, low), value)
                cols.append(value)
            result.append(jnp.concatenate(cols, axis=1))
        return result

    s_low = jnp.broadcast_to(sent_nodes & (LANES - 1), (8, LANES))
    s_high = jnp.broadcast_to(sent_nodes >> 7, (8, LANES))

    for sweep in range(SWEEPS):
        near = corners(x_ref)
        for c in range(3):
            y = mm3(smooth_parts, near[c])
            y_high = y.astype(BF16).astype(F32)
            y_ref[c * ROWS : (c + 1) * ROWS, :] = y_high
            y_ref[(3 + c) * ROWS : (4 + c) * ROWS, :] = y - y_high
        for a in range(basis):
            at = pl.ds(a * elems, elems)
            chosen = jnp.where(alive, hi_ref[a : a + 1, :], groups) == sub_hi
            for i in range(6):
                z_ref[i * groups : (i + 1) * groups, at] = jnp.where(
                    chosen, y_ref[i * ROWS + a : i * ROWS + a + 1, :], 0.0
                ).astype(BF16)
        both = mm_nt(z_ref[...], b_ref[...])
        sums = both[0 : 3 * groups] + both[3 * groups :]
        for c in range(3):
            for g in range(groups):
                r = c * groups + g
                s_ref[g * 8 + c : g * 8 + c + 1, :] = sums[r : r + 1, :]
        picked = jnp.zeros((8, LANES), F32)
        for g in range(groups):
            picked = jnp.where(s_high == g, pick(s_ref[g * 8 : g * 8 + 8, :], s_low), picked)
        v_send[sweep] = jnp.where(row < 3, picked, 0.0)
        for k in range(4):
            node_copy(sweep, k).start()
        for k in range(4):
            node_copy(sweep, k).wait_recv()
        arrived = v_recv[sweep, 0]
        for k in range(1, 4):
            arrived = jnp.where(lane // shared == k, v_recv[sweep, k], arrived)
        arr_high = arrived.astype(BF16).astype(F32)
        arr_low = arrived - arr_high
        pieces = [
            jnp.where(got_mask, part[c : c + 1, :], 0.0).astype(BF16)
            for part in (arr_high, arr_low) for c in range(3)
        ]
        both = mm_nt(jnp.concatenate(pieces, axis=0), rb_ref[...])
        sums = sums + (both[0 : 3 * groups] + both[3 * groups :])
        x_ref[...] = 0.5 * x_ref[...] + sums * half_inv

    for c in range(3):
        for g in range(groups):
            r = c * groups + g
            out_c[0, c : c + 1, g * LANES : (g + 1) * LANES] = x_ref[r : r + 1, :]

    x_ref[...] = x_ref[...] - x0_ref[...]
    near = corners(x_ref)
    projected = jnp.zeros((8, elems), F32)
    for c in range(3):
        projected = projected + mm3(split(fg_ref[c * 8 : c * 8 + 8, 0:ROWS]), near[c])
    rate = rates[0] * (1.0 + 0.5 * jnp.tanh(projected[0:faces])) * jnp.where(alive, 1.0, 0.0)
    rate_ref[0:faces, :] = rate
    most = jnp.max(jnp.sum(rate, axis=0, keepdims=True), axis=1, keepdims=True)
    m_send[0] = jnp.broadcast_to(most, (8, LANES))
    for j in range(len(partners[0]) if rounds else 0):
        most_copy(0, j).start()

    def gather_local():
        for v in range(fields):
            for h in range(halves):
                for f in range(faces):
                    which = jnp.broadcast_to(
                        neighbours[0, f : f + 1, h * LANES : (h + 1) * LANES], (ROWS, LANES)
                    )
                    low, far = which & (LANES - 1), which >> 7
                    got = pick(u_ref[v * ROWS : (v + 1) * ROWS, 0:LANES], low)
                    for s in range(1, halves):
                        other = pick(u_ref[v * ROWS : (v + 1) * ROWS, s * LANES : (s + 1) * LANES], low)
                        got = jnp.where(far == s, other, got)
                    r = (v * faces + f) * ROWS
                    nb_ref[r : r + ROWS, h * LANES : (h + 1) * LANES] = got

    def change_of(step, v):
        ghost = g_recv[step, 0]
        for k in range(1, 4):
            ghost = jnp.where(slot_of == (v + k) % slots, g_recv[step, k], ghost)
        u = u_ref[v * ROWS : (v + 1) * ROWS, :]
        stack = [u]
        for f in range(faces):
            cols = []
            r = (v * faces + f) * ROWS
            for h in range(halves):
                which = jnp.broadcast_to(
                    neighbours[0, f : f + 1, h * LANES : (h + 1) * LANES], (ROWS, LANES)
                )
                got = pick(ghost, (which + ghosts * v) & (LANES - 1))
                cols.append(jnp.where(which >= elems, got, nb_ref[r : r + ROWS, h * LANES : (h + 1) * LANES]))
            stack.append(rate_ref[f : f + 1, :] * (jnp.concatenate(cols, axis=1) - u))
        high, low = split(jnp.concatenate(stack, axis=0))
        depth = (faces + 1) * ROWS
        first = mm(w_ref[:, 0:depth], high)
        return first[0:ROWS] + (first[ROWS:] + mm(w_ref[0:ROWS, 0:depth], low))

    for step in range(STEPS):
        if step > 0:
            pack_ghosts(step)
            for k in range(4):
                ghost_copy(step, k).start()
        gather_local()
        for k in range(4):
            ghost_copy(step, k).wait_recv()
        changes = [change_of(step, v) for v in range(fields)]
        if step == 0:
            for r, one in enumerate(partners):
                if r > 0:
                    m_send[r] = jnp.broadcast_to(most, (8, LANES))
                    for j in range(len(one)):
                        most_copy(r, j).start()
                at = sum(len(p) for p in partners[:r])
                for j in range(len(one)):
                    most_copy(r, j).wait_recv()
                tile = m_send[r]
                for j in range(len(one)):
                    tile = jnp.maximum(tile, m_recv[at + j])
                most = tile[0:1, 0:1]
            scale = jnp.where(alive, CFL / most, 0.0)
        for v in range(fields):
            new = u_ref[v * ROWS : (v + 1) * ROWS, :] + scale * changes[v]
            if step < STEPS - 1:
                u_ref[v * ROWS : (v + 1) * ROWS, :] = new
            else:
                out_u[0, v] = new[0:basis, :]

    for sweep in range(SWEEPS):
        for k in range(4):
            node_copy(sweep, k).wait_send()
    for step in range(STEPS):
        for k in range(4):
            ghost_copy(step, k).wait_send()
    for r, one in enumerate(partners):
        for j in range(len(one)):
            most_copy(r, j).wait_send()


def on_device(*args):
    pos, states, conn = args[:3]
    parts = lax.axis_size("dom")
    w = max(parts // 8, 1)
    shifts = (1, -1, w, -w)
    rounds = rounds_of(parts)
    total = sum(r - 1 for r, _ in rounds)
    basis, elems = conn.shape[1:]
    fields, faces = states.shape[1], args[6].shape[1]
    groups = pos.shape[2] // LANES
    vmem = pl.BlockSpec(memory_space=pltpu.VMEM)
    smem = pl.BlockSpec(memory_space=pltpu.SMEM)
    specs = [smem if i == 7 else vmem for i in range(len(args))]
    scratch = [
        pltpu.VMEM((3 * groups, LANES), F32),
        pltpu.VMEM((3 * groups, LANES), F32),
        pltpu.VMEM((8 * groups, LANES), F32),
        pltpu.VMEM((ROWS, elems), jnp.int32),
        pltpu.VMEM((ROWS, elems), jnp.int32),
        pltpu.VMEM((6 * ROWS, elems), F32),
        pltpu.VMEM((6 * groups, basis * elems), BF16),
        pltpu.VMEM((LANES, basis * elems), BF16),
        pltpu.VMEM((LANES, LANES), BF16),
        pltpu.VMEM((fields * ROWS, elems), F32),
        pltpu.VMEM((fields * faces * ROWS, elems), F32),
        pltpu.VMEM((8, elems), F32),
        pltpu.VMEM(((faces + 1) * ROWS, LANES), F32),
        pltpu.VMEM((24, LANES), F32),
        pltpu.VMEM((2 * ROWS, 2 * LANES), BF16),
        pltpu.VMEM((24, LANES), jnp.int32),
        pltpu.VMEM((SWEEPS, 8, LANES), F32),
        pltpu.VMEM((SWEEPS, 4, 8, LANES), F32),
        pltpu.VMEM((STEPS, 4, ROWS, LANES), F32),
        pltpu.VMEM((STEPS, 4, ROWS, LANES), F32),
        pltpu.VMEM((max(len(rounds), 1), 8, LANES), F32),
        pltpu.VMEM((max(total, 1), 8, LANES), F32),
        pltpu.SemaphoreType.DMA((SWEEPS, 4)),
        pltpu.SemaphoreType.DMA((SWEEPS, 4)),
        pltpu.SemaphoreType.DMA((STEPS, 4)),
        pltpu.SemaphoreType.DMA((STEPS, 4)),
        pltpu.SemaphoreType.DMA((max(total, 1),)),
        pltpu.SemaphoreType.DMA((max(total, 1),)),
    ]
    return pl.pallas_call(
        functools.partial(kernel, parts, shifts, rounds),
        out_shape=(
            jax.ShapeDtypeStruct(pos.shape, F32),
            jax.ShapeDtypeStruct(states.shape, F32),
        ),
        in_specs=specs,
        out_specs=(vmem, vmem),
        scratch_shapes=scratch,
        compiler_params=pltpu.CompilerParams(
            collective_id=0, has_side_effects=True, vmem_limit_bytes=32 * 1024 * 1024
        ),
    )(*args)


def solution(mesh):
    dom = lambda rank: P("dom", *([None] * (rank - 1)))
    in_specs = (
        dom(3), dom(4), dom(3), dom(3), dom(3), dom(3), dom(3), P("dom"),
        P(), P(), dom(3), P(), P(), P(),
    )
    return jax.shard_map(
        on_device, mesh=mesh, in_specs=in_specs, out_specs=(dom(3), dom(4)), check_vma=False
    )
```

```python
import functools

import jax
import jax.numpy as jnp
from jax import lax
from jax.experimental import pallas as pl
from jax.experimental.pallas import tpu as pltpu
from jax.sharding import PartitionSpec as P

SWEEPS = 3
STEPS = 4
CFL = 0.4
F32 = jnp.float32
BF16 = jnp.bfloat16
HIGHEST = lax.Precision.HIGHEST
MESH = pl.DeviceIdType.MESH
LANES = 128
ROWS = 32
RADIX = 4


def rounds_of(parts):
    found, stride = [], 1
    while parts > 1:
        radix = max(r for r in range(1, RADIX + 1) if parts % r == 0)
        if radix == 1:
            radix = parts
        found.append((radix, stride))
        stride *= radix
        parts //= radix
    return found


def pick(table, index):
    return jnp.take_along_axis(table, index, axis=1, mode="promise_in_bounds")


def split(x):
    high = x.astype(BF16)
    low = (x - high.astype(F32)).astype(BF16)
    return high, low


def mm(a, b):
    return jnp.dot(a, b, preferred_element_type=F32)


def mm3(a, b):
    high, low = split(b)
    return mm(a[0], high) + (mm(a[1], high) + mm(a[0], low))


def mm_nt(a, b):
    return lax.dot_general(a, b, (((1,), (1,)), ((), ())), preferred_element_type=F32)


def iota(shape, dim):
    return lax.broadcasted_iota(jnp.int32, shape, dim)


def kernel(
    parts, shifts, rounds,
    pos, states, conn, send_nodes, recv_nodes, send_elems, neighbours, live,
    smooth, face_geo, rates, stiff, lift, mass_inv,
    out_c, out_u,
    x_ref, x0_ref, s_ref, lo_ref, hi_ref, y_ref, z_ref, b_ref, rb_ref,
    u_ref, nb_ref, rate_ref, pad_ref, fg_ref, w_ref, idx_ref,
    v_send, v_recv, g_send, g_recv, m_send, m_recv,
    vs_sem, vr_sem, gs_sem, gr_sem, ms_sem, mr_sem,
):
    me = lax.axis_index("dom")
    basis, elems = conn.shape[0], conn.shape[2]
    fields = states.shape[0]
    faces = neighbours.shape[0]
    nodes = pos.shape[2]
    groups = nodes // LANES
    halves = elems // LANES
    shared = send_nodes.shape[2]
    ghosts = send_elems.shape[2]
    slots = LANES // ghosts

    partners = []
    for radix, stride in rounds:
        digit = lax.rem(me // stride, radix)
        partners.append(
            [me + (lax.rem(digit + j, radix) - digit) * stride for j in range(1, radix)]
        )
    targets = [lax.rem(me + o + parts, parts) for o in shifts]

    barrier = pltpu.get_barrier_semaphore()
    greeted = targets + [t for one in partners for t in one]
    for t in greeted:
        pl.semaphore_signal(barrier, inc=1, device_id=(t,), device_id_type=MESH)

    u_ref[...] = jnp.zeros(u_ref.shape, F32)
    for v in range(fields):
        u_ref[v * ROWS : v * ROWS + basis, :] = states[v, :, 0, :]

    lane = iota((8, LANES), 1)
    row = iota((8, LANES), 0)
    idx_ref[...] = jnp.zeros(idx_ref.shape, jnp.int32)
    idx_ref[0:4, 0:shared] = send_nodes[0]
    idx_ref[8:12, 0:shared] = recv_nodes[0]
    idx_ref[16:20, 0:ghosts] = send_elems[0]

    def flat(block):
        spread = pick(block, lax.rem(lane, shared))
        kept = jnp.where(lane // shared == row, spread, 0)
        return jnp.sum(kept, axis=0, keepdims=True)

    sent_nodes = flat(idx_ref[0:8, :])
    got_nodes = flat(idx_ref[8:16, :])
    idx_ref[16:24, :] = pick(idx_ref[16:24, :], lax.rem(lane, ghosts))

    slot_of = iota((ROWS, LANES), 1) // ghosts

    def pack_ghosts(step):
        for k in range(4):
            which = jnp.broadcast_to(idx_ref[16 + k : 17 + k, :], (ROWS, LANES))
            low = which & (LANES - 1)
            far = which >> 7
            tile = jnp.zeros((ROWS, LANES), F32)
            for v in range(fields):
                got = pick(u_ref[v * ROWS : (v + 1) * ROWS, 0:LANES], low)
                for h in range(1, halves):
                    other = pick(u_ref[v * ROWS : (v + 1) * ROWS, h * LANES : (h + 1) * LANES], low)
                    got = jnp.where(far == h, other, got)
                tile = jnp.where(slot_of == (v + k) % slots, got, tile)
            g_send[step, k] = tile

    def ghost_copy(step, k):
        return pltpu.make_async_remote_copy(
            src_ref=g_send.at[step, k], dst_ref=g_recv.at[step, k],
            send_sem=gs_sem.at[step, k], recv_sem=gr_sem.at[step, k],
            device_id=(targets[k],), device_id_type=MESH,
        )

    def node_copy(sweep, k):
        return pltpu.make_async_remote_copy(
            src_ref=v_send.at[sweep], dst_ref=v_recv.at[sweep, k],
            send_sem=vs_sem.at[sweep, k], recv_sem=vr_sem.at[sweep, k],
            device_id=(targets[k],), device_id_type=MESH,
        )

    def most_copy(r, j):
        at = sum(len(p) for p in partners[:r]) + j
        return pltpu.make_async_remote_copy(
            src_ref=m_send.at[r], dst_ref=m_recv.at[at],
            send_sem=ms_sem.at[at], recv_sem=mr_sem.at[at],
            device_id=(partners[r][j],), device_id_type=MESH,
        )

    pack_ghosts(0)

    for c in range(3):
        for g in range(groups):
            r = c * groups + g
            x0_ref[r : r + 1, :] = pos[c, 0:1, g * LANES : (g + 1) * LANES]
    x_ref[...] = x0_ref[...]
    s_ref[...] = jnp.zeros(s_ref.shape, F32)

    alive = (iota((1, elems), 1) < live[0])
    lo_ref[...] = jnp.zeros(lo_ref.shape, jnp.int32)
    hi_ref[...] = jnp.zeros(hi_ref.shape, jnp.int32)
    lo_ref[0:basis, :] = conn[:, 0, :] & (LANES - 1)
    hi_ref[0:basis, :] = conn[:, 0, :] >> 7

    sub_lo = iota((LANES, elems), 0)
    sub_hi = iota((groups, elems), 0)
    one_lo, one_hi = jnp.float32(1.0), jnp.float32(1.0)
    for a in range(basis):
        at = pl.ds(a * elems, elems)
        b_ref[:, at] = jnp.where(sub_lo == lo_ref[a : a + 1, :], one_lo, 0.0).astype(BF16)
        z_ref[0:groups, at] = jnp.where(
            jnp.where(alive, hi_ref[a : a + 1, :], groups) == sub_hi, one_hi, 0.0
        ).astype(BF16)
    got_lo, got_hi = got_nodes & (LANES - 1), got_nodes >> 7
    rb_ref[...] = jnp.where(iota((LANES, LANES), 0) == got_lo, one_lo, 0.0).astype(BF16)
    got_mask = iota((groups, LANES), 0) == got_hi
    count = mm_nt(z_ref[0:groups, :], b_ref[...])
    count = count + mm_nt(jnp.where(got_mask, one_hi, 0.0).astype(BF16), rb_ref[...])
    half_inv = 0.5 / jnp.maximum(count, 1.0)
    half_inv = jnp.concatenate([half_inv] * 3, axis=0)

    pl.semaphore_wait(barrier, len(greeted))
    for k in range(4):
        ghost_copy(0, k).start()

    pad_ref[...] = jnp.zeros(pad_ref.shape, F32)
    for i in range(faces + 1):
        matrix = stiff[...] if i == 0 else lift[i - 1]
        pad_ref[i * ROWS : i * ROWS + basis, 0:basis] = jnp.dot(
            mass_inv[...], matrix, precision=HIGHEST, preferred_element_type=F32
        )
    wide = []
    for first in range(0, faces + 1, 4):
        total = None
        for i in range(first, min(first + 4, faces + 1)):
            block = pad_ref[i * ROWS : (i + 1) * ROWS, :]
            if i > first:
                block = pltpu.roll(block, ROWS * (i - first), 1)
            total = block if total is None else total + block
        wide.append(total)
    w_high, w_low = split(jnp.concatenate(wide, axis=1))
    w_ref[0:ROWS, :] = w_high
    w_ref[ROWS : 2 * ROWS, :] = w_low
    pad_ref[0:ROWS, :] = jnp.zeros((ROWS, LANES), F32)
    pad_ref[0:basis, 0:basis] = smooth[...]
    smooth_parts = split(pad_ref[0:ROWS, 0:ROWS])
    fg_ref[...] = jnp.zeros(fg_ref.shape, F32)
    for c in range(3):
        fg_ref[c * 8 : c * 8 + faces, 0:basis] = face_geo[:, c, :]

    def corners(table):
        result = []
        for c in range(3):
            cols = []
            for h in range(halves):
                low = lo_ref[:, h * LANES : (h + 1) * LANES]
                high = hi_ref[:, h * LANES : (h + 1) * LANES]
                value = jnp.zeros((ROWS, LANES), F32)
                for g in range(groups):
                    r = c * groups + g
                    source = jnp.broadcast_to(table[r : r + 1, :], (ROWS, LANES))
                    value = jnp.where(high == g, pick(source, low), value)
                cols.append(value)
            result.append(jnp.concatenate(cols, axis=1))
        return result

    s_low = jnp.broadcast_to(sent_nodes & (LANES - 1), (8, LANES))
    s_high = jnp.broadcast_to(sent_nodes >> 7, (8, LANES))

    for sweep in range(SWEEPS):
        near = corners(x_ref)
        for c in range(3):
            y = mm3(smooth_parts, near[c])
            y_high = y.astype(BF16).astype(F32)
            y_ref[c * ROWS : (c + 1) * ROWS, :] = y_high
            y_ref[(3 + c) * ROWS : (4 + c) * ROWS, :] = y - y_high
        for a in range(basis):
            at = pl.ds(a * elems, elems)
            chosen = jnp.where(alive, hi_ref[a : a + 1, :], groups) == sub_hi
            for i in range(6):
                z_ref[i * groups : (i + 1) * groups, at] = jnp.where(
                    chosen, y_ref[i * ROWS + a : i * ROWS + a + 1, :], 0.0
                ).astype(BF16)
        both = mm_nt(z_ref[...], b_ref[...])
        sums = both[0 : 3 * groups] + both[3 * groups :]
        for c in range(3):
            for g in range(groups):
                r = c * groups + g
                s_ref[g * 8 + c : g * 8 + c + 1, :] = sums[r : r + 1, :]
        picked = jnp.zeros((8, LANES), F32)
        for g in range(groups):
            picked = jnp.where(s_high == g, pick(s_ref[g * 8 : g * 8 + 8, :], s_low), picked)
        v_send[sweep] = jnp.where(row < 3, picked, 0.0)
        for k in range(4):
            node_copy(sweep, k).start()
        for k in range(4):
            node_copy(sweep, k).wait_recv()
        arrived = v_recv[sweep, 0]
        for k in range(1, 4):
            arrived = jnp.where(lane // shared == k, v_recv[sweep, k], arrived)
        arr_high = arrived.astype(BF16).astype(F32)
        arr_low = arrived - arr_high
        pieces = [
            jnp.where(got_mask, part[c : c + 1, :], 0.0).astype(BF16)
            for part in (arr_high, arr_low) for c in range(3)
        ]
        both = mm_nt(jnp.concatenate(pieces, axis=0), rb_ref[...])
        sums = sums + (both[0 : 3 * groups] + both[3 * groups :])
        x_ref[...] = 0.5 * x_ref[...] + sums * half_inv

    for c in range(3):
        for g in range(groups):
            r = c * groups + g
            out_c[c, 0:1, g * LANES : (g + 1) * LANES] = x_ref[r : r + 1, :]

    x_ref[...] = x_ref[...] - x0_ref[...]
    near = corners(x_ref)
    projected = jnp.zeros((8, elems), F32)
    for c in range(3):
        projected = projected + mm3(split(fg_ref[c * 8 : c * 8 + 8, 0:ROWS]), near[c])
    rate = rates[:, 0, :] * (1.0 + 0.5 * jnp.tanh(projected[0:faces])) * jnp.where(alive, 1.0, 0.0)
    rate_ref[0:faces, :] = rate
    most = jnp.max(jnp.sum(rate, axis=0, keepdims=True), axis=1, keepdims=True)
    m_send[0] = jnp.broadcast_to(most, (8, LANES))
    for j in range(len(partners[0]) if rounds else 0):
        most_copy(0, j).start()

    def gather_local():
        for v in range(fields):
            for h in range(halves):
                for f in range(faces):
                    which = jnp.broadcast_to(
                        neighbours[f, 0:1, h * LANES : (h + 1) * LANES], (ROWS, LANES)
                    )
                    low, far = which & (LANES - 1), which >> 7
                    got = pick(u_ref[v * ROWS : (v + 1) * ROWS, 0:LANES], low)
                    for s in range(1, halves):
                        other = pick(u_ref[v * ROWS : (v + 1) * ROWS, s * LANES : (s + 1) * LANES], low)
                        got = jnp.where(far == s, other, got)
                    r = (v * faces + f) * ROWS
                    nb_ref[r : r + ROWS, h * LANES : (h + 1) * LANES] = got

    def change_of(step, v):
        ghost = g_recv[step, 0]
        for k in range(1, 4):
            ghost = jnp.where(slot_of == (v + k) % slots, g_recv[step, k], ghost)
        u = u_ref[v * ROWS : (v + 1) * ROWS, :]
        stack = [u]
        for f in range(faces):
            cols = []
            r = (v * faces + f) * ROWS
            for h in range(halves):
                which = jnp.broadcast_to(
                    neighbours[f, 0:1, h * LANES : (h + 1) * LANES], (ROWS, LANES)
                )
                got = pick(ghost, (which + ghosts * v) & (LANES - 1))
                cols.append(jnp.where(which >= elems, got, nb_ref[r : r + ROWS, h * LANES : (h + 1) * LANES]))
            stack.append(rate_ref[f : f + 1, :] * (jnp.concatenate(cols, axis=1) - u))
        high, low = split(jnp.concatenate(stack, axis=0))
        depth = (faces + 1) * ROWS
        first = mm(w_ref[:, 0:depth], high)
        return first[0:ROWS] + (first[ROWS:] + mm(w_ref[0:ROWS, 0:depth], low))

    for step in range(STEPS):
        if step > 0:
            pack_ghosts(step)
            for k in range(4):
                ghost_copy(step, k).start()
        gather_local()
        for k in range(4):
            ghost_copy(step, k).wait_recv()
        changes = [change_of(step, v) for v in range(fields)]
        if step == 0:
            for r, one in enumerate(partners):
                if r > 0:
                    m_send[r] = jnp.broadcast_to(most, (8, LANES))
                    for j in range(len(one)):
                        most_copy(r, j).start()
                at = sum(len(p) for p in partners[:r])
                for j in range(len(one)):
                    most_copy(r, j).wait_recv()
                tile = m_send[r]
                for j in range(len(one)):
                    tile = jnp.maximum(tile, m_recv[at + j])
                most = tile[0:1, 0:1]
            scale = jnp.where(alive, CFL / most, 0.0)
        for v in range(fields):
            new = u_ref[v * ROWS : (v + 1) * ROWS, :] + scale * changes[v]
            if step < STEPS - 1:
                u_ref[v * ROWS : (v + 1) * ROWS, :] = new
            else:
                out_u[v, :, 0, :] = new[0:basis, :]

    for sweep in range(SWEEPS):
        for k in range(4):
            node_copy(sweep, k).wait_send()
    for step in range(STEPS):
        for k in range(4):
            ghost_copy(step, k).wait_send()
    for r, one in enumerate(partners):
        for j in range(len(one)):
            most_copy(r, j).wait_send()


def on_device(*args):
    pos, states, conn = args[:3]
    parts = lax.axis_size("dom")
    w = max(parts // 8, 1)
    shifts = (1, -1, w, -w)
    rounds = rounds_of(parts)
    total = sum(r - 1 for r, _ in rounds)
    basis, elems = conn.shape[1:]
    fields, faces = states.shape[1], args[6].shape[1]
    groups = pos.shape[2] // LANES
    vmem = pl.BlockSpec(memory_space=pltpu.VMEM)
    smem = pl.BlockSpec(memory_space=pltpu.SMEM)
    specs = [smem if i == 7 else vmem for i in range(len(args))]
    scratch = [
        pltpu.VMEM((3 * groups, LANES), F32),
        pltpu.VMEM((3 * groups, LANES), F32),
        pltpu.VMEM((8 * groups, LANES), F32),
        pltpu.VMEM((ROWS, elems), jnp.int32),
        pltpu.VMEM((ROWS, elems), jnp.int32),
        pltpu.VMEM((6 * ROWS, elems), F32),
        pltpu.VMEM((6 * groups, basis * elems), BF16),
        pltpu.VMEM((LANES, basis * elems), BF16),
        pltpu.VMEM((LANES, LANES), BF16),
        pltpu.VMEM((fields * ROWS, elems), F32),
        pltpu.VMEM((fields * faces * ROWS, elems), F32),
        pltpu.VMEM((8, elems), F32),
        pltpu.VMEM(((faces + 1) * ROWS, LANES), F32),
        pltpu.VMEM((24, LANES), F32),
        pltpu.VMEM((2 * ROWS, 2 * LANES), BF16),
        pltpu.VMEM((24, LANES), jnp.int32),
        pltpu.VMEM((SWEEPS, 8, LANES), F32),
        pltpu.VMEM((SWEEPS, 4, 8, LANES), F32),
        pltpu.VMEM((STEPS, 4, ROWS, LANES), F32),
        pltpu.VMEM((STEPS, 4, ROWS, LANES), F32),
        pltpu.VMEM((max(len(rounds), 1), 8, LANES), F32),
        pltpu.VMEM((max(total, 1), 8, LANES), F32),
        pltpu.SemaphoreType.DMA((SWEEPS, 4)),
        pltpu.SemaphoreType.DMA((SWEEPS, 4)),
        pltpu.SemaphoreType.DMA((STEPS, 4)),
        pltpu.SemaphoreType.DMA((STEPS, 4)),
        pltpu.SemaphoreType.DMA((max(total, 1),)),
        pltpu.SemaphoreType.DMA((max(total, 1),)),
    ]
    rowed = [
        a.reshape(a.shape[1:-1] + (1, a.shape[-1])) if i in (0, 1, 2, 6, 10) else a
        for i, a in enumerate(args)
    ]
    new_c, new_u = pl.pallas_call(
        functools.partial(kernel, parts, shifts, rounds),
        out_shape=(
            jax.ShapeDtypeStruct(rowed[0].shape, F32),
            jax.ShapeDtypeStruct(rowed[1].shape, F32),
        ),
        in_specs=specs,
        out_specs=(vmem, vmem),
        scratch_shapes=scratch,
        compiler_params=pltpu.CompilerParams(
            collective_id=0, has_side_effects=True, vmem_limit_bytes=32 * 1024 * 1024
        ),
    )(*rowed)
    return new_c.reshape(pos.shape), new_u.reshape(states.shape)


def solution(mesh):
    dom = lambda rank: P("dom", *([None] * (rank - 1)))
    in_specs = (
        dom(3), dom(4), dom(3), dom(3), dom(3), dom(3), dom(3), P("dom"),
        P(), P(), dom(3), P(), P(), P(),
    )
    return jax.shard_map(
        on_device, mesh=mesh, in_specs=in_specs, out_specs=(dom(3), dom(4)), check_vma=False
    )
```
